32 devices in a mesh: rows: 4 (over y, x), past: 8 (over z, core).
Axes of the slice: x: 2, y: 2, z: 4, core: 2. Of those that a mesh axis runs over, the one named last changes fastest.
Arguments:
- tile_left: float32 [4, 8, 1024, 128], P('rows', 'past'), may hold values from -0.1875 to 0.1875
- tile_right: float32 [4, 8, 1024, 128], P('rows', 'past'), may hold values from -0.1875 to 0.1875
- diag_left: float32 [8, 1024, 128], P('past', 'rows'), may hold values from -6 to 6
- diag_right: float32 [8, 1024, 128], P('past', 'rows'), may hold values from -0.1875 to 0.1875
- present: int32 [4, 8], P('rows', 'past'), may hold values 0 or 1
- old_left: float32 [4, 1024, 128], P('rows'), may hold values from -6 to 6
- old_right: float32 [4, 1024, 128], P('rows'), may hold values from -0.1875 to 0.1875
- start: float32 [4, 1024, 128], P('rows'), may hold values from -6 to 6
Outputs:
- left: float32 [4, 1024, 128], P('rows')
- right: float32 [4, 1024, 128], P('rows')
The draws below stay inside these ranges and needn't reach their ends.
Inputs may be any that keep to these rules, and one draw needn't show every extreme that they name: present is 1 exactly where the past tile of that tile row and panel is listed.
All inputs are finite; a program needn't handle non-finite values. No bound on the sum of `present` on one device may be relied on, other than what follows from the above.
Results may differ from the reference program's by a relative error of at most 0.00026.
Values sent between devices are 32-bit elements; how exact they have to be, the bound alone decides.
A program may use at most 64 MiB of HBM per device.

```python
import math
import jax
import jax.numpy as jnp
from jax import lax

B = 1024
R = 128
ITERS = 3
TROWS = 4
PAST = 8


def set_ends(drawn, key, smallest, top_value):
    longest = drawn.shape.index(max(drawn.shape))
    spots = []
    for shift in (0, 1):
        where = [jax.random.randint(jax.random.fold_in(key, axis), (), 0, length) for axis, length in enumerate(drawn.shape)]
        where[longest] = (where[longest] + shift) % drawn.shape[longest]
        spots.append(tuple(where))
    return drawn.at[spots[0]].set(smallest).at[spots[1]].set(top_value)


def levels(own_key, extent, cuts, low, largest):
    loudness = 1.0
    for dim, blocks in cuts:
        heights = jax.random.uniform(jax.random.fold_in(jax.random.fold_in(own_key, 6), dim), (blocks,), jnp.float32, low / len(cuts), largest / len(cuts))
        loudness = loudness * jnp.repeat(jnp.exp(heights), extent[dim] // blocks).reshape((-1,) + (1,) * (len(extent) - 1 - dim))
    return loudness


def centred(own_key, dims, scale, most, split=(), kind=jnp.bfloat16):
    factor_of = levels(own_key, dims, split, -0.22, 0.18) if split else 1.0
    entries = jax.random.normal(own_key, dims, jnp.float32) * scale * factor_of
    return jnp.minimum(jnp.maximum(entries, -most), most).astype(kind)


def setup_inputs(seed: int = 0) -> dict:
    splits = jax.random.split(jax.random.key(seed), 9)
    return {
        "tile_left": centred(splits[0], (TROWS, PAST, B, R), (R * PAST) ** -0.5, 0.1875, ((0, 4), (1, 8)), jnp.float32),
        "tile_right": centred(splits[1], (TROWS, PAST, B, R), B ** -0.5, 0.1875, ((0, 4), (1, 8)), jnp.float32),
        "diag_left": centred(splits[2], (PAST, B, R), 1.0, 6.0, ((0, 8), (1, 4)), jnp.float32),
        "diag_right": centred(splits[3], (PAST, B, R), B ** -0.5, 0.1875, ((0, 8), (1, 4)), jnp.float32),
        "present": set_ends((jax.random.randint(splits[4], (TROWS, PAST), 0, 4) < 3).astype(jnp.int32), jax.random.fold_in(splits[4], 1), 0, 1),
        "old_left": centred(splits[5], (TROWS, B, R), 1.0, 6.0, ((0, 4),), jnp.float32),
        "old_right": centred(splits[6], (TROWS, B, R), (8 * R) ** -0.5, 0.1875, ((0, 4),), jnp.float32),
        "start": centred(splits[7], (TROWS, B, R), 1.0, 6.0, ((0, 4),), jnp.float32),
    }


HIGH = lax.Precision.HIGHEST

def orthonormal(block):
    gram = jnp.dot(block.T, block, precision=HIGH)
    lower = jnp.linalg.cholesky(gram)
    inverse = jax.scipy.linalg.solve_triangular(lower, jnp.eye(block.shape[1], dtype=jnp.float32), lower=True)
    return jnp.dot(block, inverse.T, precision=HIGH)

def reference(tile_left, tile_right, diag_left, diag_right, present, old_left, old_right, start):
    weights = present.astype(jnp.float32)

    def one_row(items):
        left_row, right_row, mask_row, old_l, old_r, begin = items
        coupling = jnp.einsum('pbr,pbs->prs', right_row, diag_right, precision=HIGH) * mask_row[:, None, None]

        def forward(block):
            inner = jnp.einsum('pbs,bt->pst', diag_left, block, precision=HIGH)
            middle = jnp.einsum('prs,pst->prt', coupling, inner, precision=HIGH)
            summed = jnp.einsum('pbr,prt->bt', left_row, middle, precision=HIGH)
            return jnp.dot(old_l, jnp.dot(old_r.T, block, precision=HIGH), precision=HIGH) - summed

        def backward(block):
            inner = jnp.einsum('pbr,bt->prt', left_row, block, precision=HIGH)
            middle = jnp.einsum('prs,prt->pst', coupling, inner, precision=HIGH)
            summed = jnp.einsum('pbs,pst->bt', diag_left, middle, precision=HIGH)
            return jnp.dot(old_r, jnp.dot(old_l.T, block, precision=HIGH), precision=HIGH) - summed
        basis = orthonormal(forward(begin))
        for sweep in range(ITERS):
            basis = orthonormal(forward(orthonormal(backward(basis))))
        return (basis * math.sqrt(B), backward(basis))
    return lax.map(one_row, (tile_left, tile_right, weights, old_left, old_right, start))
```

```python
import functools
import math

import jax
import jax.numpy as jnp
from jax import lax
from jax.experimental import pallas as pl
from jax.experimental.pallas import tpu as pltpu
from jax.sharding import PartitionSpec as P

ITERS = 3
HIGH = lax.Precision.HIGHEST
F32 = jnp.float32
BF16 = jnp.bfloat16
NN = (((1,), (0,)), ((), ()))
NT = (((1,), (1,)), ((), ()))
TN = (((0,), (0,)), ((), ()))


def halves(value):
    high = value.astype(BF16)
    return high, (value - high.astype(F32)).astype(BF16)


def dot(left, right, dims, precision=None):
    return lax.dot_general(left, right, dims, precision=precision, preferred_element_type=F32)


def wide_nt(left, right):
    lh, ll = halves(left)
    rh, rl = halves(right)
    return dot(jnp.concatenate([lh, lh, ll], 1), jnp.concatenate([rh, rl, rh], 1), NT)


def lower_inverse(gram):
    size = gram.shape[0]
    rows = [gram[8 * b : 8 * b + 8] for b in range(size // 8)]
    lane = lax.broadcasted_iota(jnp.int32, (8, size), 1)
    sub = lax.broadcasted_iota(jnp.int32, (8, size), 0)
    for k in range(size):
        own, s = divmod(k, 8)
        pivot_row = rows[own][s : s + 1]
        inverse = 1.0 / pivot_row[:, k : k + 1]
        at_pivot = lane == k
        scaled = jnp.broadcast_to(
            jnp.where(lane[:1] == k, 1.0, pivot_row) * inverse, (8, size)
        )
        for b in range(own, size // 8):
            if b == own and s == 7:
                continue
            factor = jnp.broadcast_to(rows[b][:, k : k + 1], (8, size))
            fresh = jnp.where(at_pivot, 0.0, rows[b]) - factor * scaled
            rows[b] = jnp.where(sub > s, fresh, rows[b]) if b == own else fresh
    out = []
    for b in range(size // 8):
        diagonal = lane == sub + 8 * b
        pivot = jnp.sum(jnp.where(diagonal, rows[b], 0.0), axis=1, keepdims=True)
        unit = jnp.where(lane < sub + 8 * b, rows[b], jnp.where(diagonal, 1.0, 0.0))
        out.append(unit * lax.rsqrt(pivot))
    return jnp.concatenate(out, 0)


def split_into(total_ref, high_ref, low_ref, index):
    order = total_ref.shape[0]
    tile = 128

    def body(t, carry):
        at = pl.ds(pl.multiple_of(t * tile, tile), tile)
        high, low = halves(total_ref[at, :])
        high_ref[index, at, :] = high
        low_ref[index, at, :] = low
        return carry

    lax.fori_loop(0, order // tile, body, 0)


def apply_matrix(high_ref, low_ref, index, block, out_ref):
    order, width = block.shape
    bh, bl = halves(block)
    both = jnp.concatenate([bh, bl], 1)
    tile = 256

    def body(t, carry):
        at = pl.ds(pl.multiple_of(t * tile, tile), tile)
        first = dot(high_ref[index, at, :], both, NN)
        second = dot(low_ref[index, at, :], bh, NN)
        out_ref[at, :] = first[:, :width] + (first[:, width:] + second)
        return carry

    lax.fori_loop(0, order // tile, body, 0)


def iterate(high_ref, low_ref, block_ref, left_ref, right_ref):
    order, width = block_ref.shape

    def step(t, carry):
        apply_matrix(high_ref, low_ref, lax.rem(t, 2), block_ref[...], right_ref)
        value = right_ref[...]
        inverse = lower_inverse(dot(value, value, TN, HIGH))
        block_ref[...] = dot(value, inverse, NT, HIGH)
        return carry

    lax.fori_loop(0, 2 * ITERS + 1, step, 0)
    left_ref[...] = block_ref[...] * math.sqrt(order)
    apply_matrix(high_ref, low_ref, 1, block_ref[...], right_ref)


def local_kernel(past_ref, old_left_ref, old_right_ref, start_ref, left_ref, right_ref, total, high, low, block):
    order = start_ref.shape[0]
    tile = 128
    block[...] = start_ref[...]
    old_left = old_left_ref[...]
    old_right = old_right_ref[...]

    def body(t, carry):
        at = pl.ds(pl.multiple_of(t * tile, tile), tile)
        total[at, :] = wide_nt(old_left_ref[at, :], old_right) - past_ref[at, :]
        return carry

    lax.fori_loop(0, order // tile, body, 0)
    split_into(total, high, low, 0)
    total[...] = total[...].T
    split_into(total, high, low, 1)
    iterate(high, low, block, left_ref, right_ref)


def shards(tile_left, tile_right, diag_left, diag_right, present, old_left, old_right, start):
    diag_left = lax.all_gather(diag_left[0], "rows", axis=0, tiled=True)
    diag_right = lax.all_gather(diag_right[0], "rows", axis=0, tiled=True)
    coupling = jnp.dot(tile_right[0, 0].T, diag_right, precision=HIGH) * present[0, 0].astype(F32)
    middle = jnp.dot(tile_left[0, 0], coupling, precision=HIGH)
    past = lax.psum(jnp.dot(middle, diag_left.T, precision=HIGH), "past")
    order, width = start.shape[1:]
    shape = jax.ShapeDtypeStruct((order, width), F32)
    vmem = pl.BlockSpec(memory_space=pltpu.VMEM)
    left, right = pl.pallas_call(
        local_kernel,
        out_shape=(shape, shape),
        in_specs=[vmem] * 4,
        out_specs=(vmem, vmem),
        scratch_shapes=[
            pltpu.VMEM((order, order), F32),
            pltpu.VMEM((2, order, order), BF16),
            pltpu.VMEM((2, order, order), BF16),
            pltpu.VMEM((order, width), F32),
        ],
        compiler_params=pltpu.CompilerParams(vmem_limit_bytes=48 * 2**20),
    )(past, old_left[0], old_right[0], start[0])
    return left[None], right[None]


def solution(mesh):
    placed = (
        P("rows", "past", None, None),
        P("rows", "past", None, None),
        P("past", "rows", None),
        P("past", "rows", None),
        P("rows", "past"),
        P("rows", None, None),
        P("rows", None, None),
        P("rows", None, None),
    )
    return jax.shard_map(
        shards,
        mesh=mesh,
        in_specs=placed,
        out_specs=(P("rows", None, None), P("rows", None, None)),
        check_vma=False,
    )
```

```python
import functools
import math

import jax
import jax.numpy as jnp
from jax import lax
from jax.experimental import pallas as pl
from jax.experimental.pallas import tpu as pltpu
from jax.sharding import PartitionSpec as P

ITERS = 3
HIGH = lax.Precision.HIGHEST
F32 = jnp.float32
BF16 = jnp.bfloat16
MESH = pl.DeviceIdType.MESH
NN = (((1,), (0,)), ((), ()))
NT = (((1,), (1,)), ((), ()))
TN = (((0,), (0,)), ((), ()))


def halves(value):
    high = value.astype(BF16)
    return high, (value - high.astype(F32)).astype(BF16)


def dot(left, right, dims, precision=None):
    return lax.dot_general(left, right, dims, precision=precision, preferred_element_type=F32)


def wide_nt(left, right):
    lh, ll = halves(left)
    rh, rl = halves(right)
    return dot(jnp.concatenate([lh, lh, ll], 1), jnp.concatenate([rh, rl, rh], 1), NT)


def lower_inverse(gram):
    size = gram.shape[0]
    rows = [gram[8 * b : 8 * b + 8] for b in range(size // 8)]
    lane = lax.broadcasted_iota(jnp.int32, (8, size), 1)
    sub = lax.broadcasted_iota(jnp.int32, (8, size), 0)
    for k in range(size):
        own, s = divmod(k, 8)
        pivot_row = rows[own][s : s + 1]
        inverse = 1.0 / pivot_row[:, k : k + 1]
        at_pivot = lane == k
        scaled = jnp.broadcast_to(
            jnp.where(lane[:1] == k, 1.0, pivot_row) * inverse, (8, size)
        )
        for b in range(own, size // 8):
            if b == own and s == 7:
                continue
            factor = jnp.broadcast_to(rows[b][:, k : k + 1], (8, size))
            fresh = jnp.where(at_pivot, 0.0, rows[b]) - factor * scaled
            rows[b] = jnp.where(sub > s, fresh, rows[b]) if b == own else fresh
    out = []
    for b in range(size // 8):
        diagonal = lane == sub + 8 * b
        pivot = jnp.sum(jnp.where(diagonal, rows[b], 0.0), axis=1, keepdims=True)
        unit = jnp.where(lane < sub + 8 * b, rows[b], jnp.where(diagonal, 1.0, 0.0))
        out.append(unit * lax.rsqrt(pivot))
    return jnp.concatenate(out, 0)


def split_into(total_ref, high_ref, low_ref, index):
    order = total_ref.shape[0]
    tile = 128

    def body(t, carry):
        at = pl.ds(pl.multiple_of(t * tile, tile), tile)
        high, low = halves(total_ref[at, :])
        high_ref[index, at, :] = high
        low_ref[index, at, :] = low
        return carry

    lax.fori_loop(0, order // tile, body, 0)


def apply_matrix(high_ref, low_ref, index, block, out_ref):
    order, width = block.shape
    bh, bl = halves(block)
    both = jnp.concatenate([bh, bl], 1)
    tile = 256

    def body(t, carry):
        at = pl.ds(pl.multiple_of(t * tile, tile), tile)
        first = dot(high_ref[index, at, :], both, NN)
        second = dot(low_ref[index, at, :], bh, NN)
        out_ref[at, :] = first[:, :width] + (first[:, width:] + second)
        return carry

    lax.fori_loop(0, order // tile, body, 0)


def iterate(high_ref, low_ref, block_ref, left_ref, right_ref):
    order, width = block_ref.shape

    def step(t, carry):
        apply_matrix(high_ref, low_ref, lax.rem(t, 2), block_ref[...], right_ref)
        value = right_ref[...]
        inverse = lower_inverse(dot(value, value, TN, HIGH))
        block_ref[...] = dot(value, inverse, NT, HIGH)
        return carry

    lax.fori_loop(0, 2 * ITERS + 1, step, 0)
    left_ref[...] = block_ref[...] * math.sqrt(order)
    apply_matrix(high_ref, low_ref, 1, block_ref[...], right_ref)


def accumulate(total_ref, left_ref, right_ref, first):
    order = left_ref.shape[0]
    tile = 256
    for index, (one, other) in enumerate(((left_ref, right_ref), (right_ref, left_ref))):
        oh, ol = halves(other[...])
        wide = jnp.concatenate([oh, ol, oh], 1)

        def body(t, carry):
            at = pl.ds(pl.multiple_of(t * tile, tile), tile)
            high, low = halves(one[at, :])
            value = dot(jnp.concatenate([high, high, low], 1), wide, NT)
            total_ref[index, at, :] = value if first else total_ref[index, at, :] - value
            return carry

        lax.fori_loop(0, order // tile, body, 0)


def gather_kernel(
    rows, past, tile_left, tile_right, diag_left, diag_right, weight, old_left, old_right, high, low,
    pbuf, dbuf, full, total,
    s_full, r_full, s_zd, r_zd, s_zp, r_zp, s_xd, r_xd, s_cp, r_cp, s_cd, r_cd,
):
    row = lax.axis_index("rows")
    me = lax.axis_index("past")
    core = lax.rem(me, 2)
    chip = me // 2
    chips = past // 2
    partner = me + 1 - 2 * core
    depth = diag_left.shape[0]
    peers = range(1, rows)

    def peer(d):
        return {"rows": lax.rem(row + d, rows), "past": me}

    def column(p):
        return {"rows": row, "past": p}

    barrier = pltpu.get_barrier_semaphore()
    for d in peers:
        pl.semaphore_signal(barrier, inc=1, device_id=peer(d), device_id_type=MESH)
    pl.semaphore_signal(barrier, inc=1, device_id=column(partner), device_id_type=MESH)

    @pl.when(chip > 0)
    def _():
        pl.semaphore_signal(barrier, inc=1, device_id=column(me - 2), device_id_type=MESH)

    @pl.when(chip < chips - 1)
    def _():
        pl.semaphore_signal(barrier, inc=1, device_id=column(me + 2), device_id_type=MESH)

    edge = jnp.logical_or(chip == 0, chip == chips - 1)

    @pl.when(edge)
    def _():
        pl.semaphore_wait(barrier, rows + min(chips - 1, 1))

    @pl.when(jnp.logical_not(edge))
    def _():
        pl.semaphore_wait(barrier, rows + 2)

    def send(src, dst, send_sem, recv_sem, device):
        return pltpu.make_async_remote_copy(
            src_ref=src, dst_ref=dst, send_sem=send_sem, recv_sem=recv_sem, device_id=device, device_id_type=MESH
        )

    def part(r):
        return pl.ds(pl.multiple_of(r * depth, depth), depth)

    def panel(src):
        return 2 * src + core

    def z_diag(src, way, own):
        piece = dbuf.at[panel(src), part(row)]
        return send(diag_left if own else piece, piece, s_zd.at[src, way], r_zd.at[src], column(me + 4 * way - 2))

    def z_tile(src, way):
        piece = pbuf.at[panel(src)]
        return send(piece, piece, s_zp.at[src, way], r_zp.at[src], column(me + 4 * way - 2))

    def x_diag(src, d, own):
        piece = dbuf.at[panel(src), part(row)]
        return send(diag_left if own else piece, piece, s_xd.at[src, d - 1], r_xd.at[src, d - 1], peer(d))

    def x_arrived(src, d):
        piece = dbuf.at[panel(src), part(lax.rem(row + rows - d, rows))]
        return send(piece, piece, s_xd.at[src, d - 1], r_xd.at[src, d - 1], peer(d))

    def c_tile(src, index):
        piece = pbuf.at[index]
        return send(piece, piece, s_cp.at[src], r_cp.at[src], column(partner))

    def c_diag(src, index):
        piece = dbuf.at[index]
        return send(piece, piece, s_cd.at[src], r_cd.at[src], column(partner))

    def onward(act, src, step):
        if step >= 0:

            @pl.when(chip < chips - 1)
            def _():
                act(src, 1)

        if step <= 0:

            @pl.when(chip > 0)
            def _():
                act(src, 0)

    def sources(distance):
        return ((chip, 0),) if distance == 0 else ((chip - distance, distance), (chip + distance, -distance))

    def valid(src):
        return jnp.logical_and(src >= 0, src < chips)

    def each(distance, act):
        for src, step in sources(distance):
            if distance == 0:
                act(src, step)
            else:

                @pl.when(valid(src))
                def _():
                    act(src, step)

    def spread_diag(src, step):
        own = step == 0
        if not own:
            z_diag(src, 0, False).wait_recv()
        onward(lambda s, way: z_diag(s, way, own).start(), src, step)
        for d in peers:
            x_diag(src, d, own).start()

    def spread_tile(src, step):
        if step != 0:
            z_tile(src, 0).wait_recv()
        onward(lambda s, way: z_tile(s, way).start(), src, step)
        c_tile(src, panel(src)).start()

    def complete_diag(src, step):
        for d in peers:
            x_arrived(src, d).wait_recv()
        c_diag(src, panel(src)).start()

    def add(src, step):
        accumulate(total, pbuf.at[panel(src)], dbuf.at[panel(src)], False)
        other = 2 * src + 1 - core
        c_tile(src, other).wait_recv()
        c_diag(src, other).wait_recv()
        accumulate(total, pbuf.at[other], dbuf.at[other], False)

    def finish(src, step):
        onward(lambda s, way: z_diag(s, way, step == 0).wait_send(), src, step)
        onward(lambda s, way: z_tile(s, way).wait_send(), src, step)
        for d in peers:
            x_diag(src, d, step == 0).wait_send()
        c_tile(src, panel(src)).wait_send()
        c_diag(src, panel(src)).wait_send()

    for d in peers:
        send(diag_right, full.at[part(row)], s_full.at[d - 1], r_full.at[d - 1], peer(d)).start()
    each(0, spread_diag)
    dbuf[me, part(row), :] = diag_left[...]
    full[part(row), :] = diag_right[...]
    for d in peers:
        source = full.at[part(lax.rem(row + rows - d, rows))]
        send(source, source, s_full.at[d - 1], r_full.at[d - 1], peer(d)).wait_recv()
    coupling = dot(tile_right[...], full[...], TN, HIGH) * weight[...]
    pbuf[me] = dot(tile_left[...], coupling, NN, HIGH)
    each(0, spread_tile)
    accumulate(total, old_left, old_right, True)
    each(0, complete_diag)
    for distance in range(1, chips):
        each(distance, spread_diag)
        each(distance, spread_tile)
        each(distance - 1, add)
        each(distance, complete_diag)
    each(chips - 1, add)
    split_into(total.at[0], high, low, 0)
    split_into(total.at[1], high, low, 1)
    for d in peers:
        send(diag_right, full.at[part(row)], s_full.at[d - 1], r_full.at[d - 1], peer(d)).wait_send()
    for distance in range(chips):
        each(distance, finish)


def local_kernel(high, low, start_ref, left_ref, right_ref, block):
    block[...] = start_ref[...]
    iterate(high, low, block, left_ref, right_ref)


def gathered(mesh_shape, tile_left, tile_right, diag_left, diag_right, weight, old_left, old_right):
    rows, past = mesh_shape["rows"], mesh_shape["past"]
    order, width = tile_left.shape
    vmem = pl.BlockSpec(memory_space=pltpu.VMEM)
    shape = jax.ShapeDtypeStruct((2, order, order), BF16)
    dma = pltpu.SemaphoreType.DMA
    chips = past // 2
    return pl.pallas_call(
        functools.partial(gather_kernel, rows, past),
        out_shape=(shape, shape),
        in_specs=[vmem] * 7,
        out_specs=(vmem, vmem),
        scratch_shapes=[
            pltpu.VMEM((past, order, width), F32),
            pltpu.VMEM((past, order, width), F32),
            pltpu.VMEM((order, width), F32),
            pltpu.VMEM((2, order, order), F32),
            dma((rows - 1,)), dma((rows - 1,)),
            dma((chips, 2)), dma((chips,)),
            dma((chips, 2)), dma((chips,)),
            dma((chips, rows - 1)), dma((chips, rows - 1)),
            dma((chips,)), dma((chips,)),
            dma((chips,)), dma((chips,)),
        ],
        compiler_params=pltpu.CompilerParams(
            collective_id=0, has_side_effects=True, vmem_limit_bytes=56 * 2**20
        ),
    )(tile_left, tile_right, diag_left, diag_right, weight, old_left, old_right)


def summed(tile_left, tile_right, diag_left, diag_right, weight, old_left, old_right):
    diag_left = lax.all_gather(diag_left, "rows", axis=0, tiled=True)
    diag_right = lax.all_gather(diag_right, "rows", axis=0, tiled=True)
    coupling = jnp.dot(tile_right.T, diag_right, precision=HIGH) * weight[0, 0]
    middle = jnp.dot(tile_left, coupling, precision=HIGH)
    past = lax.psum(jnp.dot(middle, diag_left.T, precision=HIGH), "past")
    total = jnp.dot(old_left, old_right.T, precision=HIGH) - past
    return halves(jnp.stack([total, total.T]))


def shards(mesh_shape, tile_left, tile_right, diag_left, diag_right, present, old_left, old_right, start):
    order, width = start.shape[1:]
    past = mesh_shape["past"]
    weight = jnp.broadcast_to(present.astype(F32), (1, width))
    terms = (tile_left[0, 0], tile_right[0, 0], diag_left[0], diag_right[0], weight, old_left[0], old_right[0])
    if past % 2 == 0 and mesh_shape["rows"] > 1 and 8 * past * order * width <= 16 * 2**20:
        high, low = gathered(mesh_shape, *terms)
    else:
        high, low = summed(*terms)
    shape = jax.ShapeDtypeStruct((order, width), F32)
    vmem = pl.BlockSpec(memory_space=pltpu.VMEM)
    left, right = pl.pallas_call(
        local_kernel,
        out_shape=(shape, shape),
        in_specs=[vmem] * 3,
        out_specs=(vmem, vmem),
        scratch_shapes=[pltpu.VMEM((order, width), F32)],
        compiler_params=pltpu.CompilerParams(vmem_limit_bytes=48 * 2**20),
    )(high, low, start[0])
    return left[None], right[None]


def solution(mesh):
    placed = (
        P("rows", "past", None, None),
        P("rows", "past", None, None),
        P("past", "rows", None),
        P("past", "rows", None),
        P("rows", "past"),
        P("rows", None, None),
        P("rows", None, None),
        P("rows", None, None),
    )
    return jax.shard_map(
        functools.partial(shards, dict(mesh.shape)),
        mesh=mesh,
        in_specs=placed,
        out_specs=(P("rows", None, None), P("rows", None, None)),
        check_vma=False,
    )
```

```python
import functools
import math

import jax
import jax.numpy as jnp
from jax import lax
from jax.experimental import pallas as pl
from jax.experimental.pallas import tpu as pltpu
from jax.sharding import PartitionSpec as P

ITERS = 3
HIGH = lax.Precision.HIGHEST
F32 = jnp.float32
BF16 = jnp.bfloat16
MESH = pl.DeviceIdType.MESH
NN = (((1,), (0,)), ((), ()))
NT = (((1,), (1,)), ((), ()))
TN = (((0,), (0,)), ((), ()))


def halves(value):
    high = value.astype(BF16)
    return high, (value - high.astype(F32)).astype(BF16)


def dot(left, right, dims, precision=None):
    return lax.dot_general(left, right, dims, precision=precision, preferred_element_type=F32)


def wide_nt(left, right):
    lh, ll = halves(left)
    rh, rl = halves(right)
    return dot(jnp.concatenate([lh, lh, ll], 1), jnp.concatenate([rh, rl, rh], 1), NT)


def lower_inverse(gram):
    size = gram.shape[0]
    step = 8
    lane = lax.broadcasted_iota(jnp.int32, (step, size), 1)
    sub = lax.broadcasted_iota(jnp.int32, (step, size), 0)
    rows = [gram[step * b : step * (b + 1)] for b in range(size // step)]
    out = []

    def all_rows(value, i):
        return jnp.broadcast_to(value[i : i + 1], (step, size))

    def all_lanes(value, k):
        return jnp.broadcast_to(value[:, k : k + 1], (step, size))

    for b in range(size // step):
        base = step * b
        own = rows[b]
        inside = jnp.logical_and(lane >= base, lane < base + step)
        start = jnp.where(inside, jnp.where(lane - base == sub, 1.0, 0.0), own)
        begun = [all_rows(start, k) for k in range(step)]
        columns = [all_lanes(own, base + k) for k in range(step)]
        a = {(i, k): all_rows(columns[k], i) for k in range(step) for i in range(k, step)}
        n = {}
        for k in range(step):
            root = lax.rsqrt(a[k, k])
            for j in range(k):
                n[k, j] = n[k, j] * root
            n[k, k] = root
            scaled = {i: a[i, k] * root for i in range(k + 1, step)}
            for i in range(k + 1, step):
                for j in range(k + 1, i + 1):
                    a[i, j] = a[i, j] - scaled[i] * scaled[j]
                for j in range(k):
                    n[i, j] = n[i, j] - scaled[i] * n[k, j]
                n[i, k] = -scaled[i] * root
        done = []
        for m in range(step):
            value = n[m, 0] * begun[0]
            for j in range(1, m + 1):
                value = value + n[m, j] * begun[j]
            done.append(value)
        own = done[0]
        for m in range(1, step):
            own = jnp.where(sub == m, done[m], own)
        out.append(jnp.where(lane < base + step, own, 0.0))
        if b + 1 == size // step:
            break
        solved = []
        for k in range(step):
            value = n[k, k] * done[k]
            for m in range(k + 1, step):
                value = value + n[m, k] * done[m]
            solved.append(value)
        for t in range(b + 1, size // step):
            value = all_lanes(rows[t], base) * solved[0]
            for k in range(1, step):
                value = value + all_lanes(rows[t], base + k) * solved[k]
            rows[t] = jnp.where(inside, 0.0, rows[t]) - value
    return jnp.concatenate(out, 0)


def split_into(total_ref, high_ref, low_ref, index):
    order = total_ref.shape[0]
    tile = 128

    def body(t, carry):
        at = pl.ds(pl.multiple_of(t * tile, tile), tile)
        high, low = halves(total_ref[at, :])
        high_ref[index, at, :] = high
        low_ref[index, at, :] = low
        return carry

    lax.fori_loop(0, order // tile, body, 0)


def apply_matrix(high_ref, low_ref, index, block, out_ref):
    order, width = block.shape
    bh, bl = halves(block)
    both = jnp.concatenate([bh, bl], 1)
    tile = 256

    def body(t, carry):
        at = pl.ds(pl.multiple_of(t * tile, tile), tile)
        first = dot(high_ref[index, at, :], both, NN)
        second = dot(low_ref[index, at, :], bh, NN)
        out_ref[at, :] = first[:, :width] + (first[:, width:] + second)
        return carry

    lax.fori_loop(0, order // tile, body, 0)


def iterate(high_ref, low_ref, block_ref, left_ref, right_ref):
    order, width = block_ref.shape

    def step(t, carry):
        apply_matrix(high_ref, low_ref, lax.rem(t, 2), block_ref[...], right_ref)
        value = right_ref[...]
        inverse = lower_inverse(dot(value, value, TN, HIGH))
        block_ref[...] = wide_nt(value, inverse)
        return carry

    lax.fori_loop(0, 2 * ITERS + 1, step, 0)
    left_ref[...] = block_ref[...] * math.sqrt(order)
    apply_matrix(high_ref, low_ref, 1, block_ref[...], right_ref)


def accumulate(total_ref, left_ref, right_ref, first):
    order = left_ref.shape[0]
    tile = 256
    for index, (one, other) in enumerate(((left_ref, right_ref), (right_ref, left_ref))):
        oh, ol = halves(other[...])
        wide = jnp.concatenate([oh, ol, oh], 1)

        def body(t, carry):
            at = pl.ds(pl.multiple_of(t * tile, tile), tile)
            high, low = halves(one[at, :])
            value = dot(jnp.concatenate([high, high, low], 1), wide, NT)
            total_ref[index, at, :] = value if first else total_ref[index, at, :] - value
            return carry

        lax.fori_loop(0, order // tile, body, 0)


def gather_kernel(
    rows, past, tile_left, tile_right, diag_left, diag_right, weight, old_left, old_right, high, low,
    pbuf, dbuf, full, total,
    s_full, r_full, s_zd, r_zd, s_zp, r_zp, s_xd, r_xd, s_cp, r_cp, s_cd, r_cd,
):
    row = lax.axis_index("rows")
    me = lax.axis_index("past")
    core = lax.rem(me, 2)
    chip = me // 2
    chips = past // 2
    partner = me + 1 - 2 * core
    depth = diag_left.shape[0]
    peers = range(1, rows)

    def peer(d):
        return {"rows": lax.rem(row + d, rows), "past": me}

    def column(p):
        return {"rows": row, "past": p}

    barrier = pltpu.get_barrier_semaphore()
    for d in peers:
        pl.semaphore_signal(barrier, inc=1, device_id=peer(d), device_id_type=MESH)
    pl.semaphore_signal(barrier, inc=1, device_id=column(partner), device_id_type=MESH)

    @pl.when(chip > 0)
    def _():
        pl.semaphore_signal(barrier, inc=1, device_id=column(me - 2), device_id_type=MESH)

    @pl.when(chip < chips - 1)
    def _():
        pl.semaphore_signal(barrier, inc=1, device_id=column(me + 2), device_id_type=MESH)

    edge = jnp.logical_or(chip == 0, chip == chips - 1)

    @pl.when(edge)
    def _():
        pl.semaphore_wait(barrier, rows + min(chips - 1, 1))

    @pl.when(jnp.logical_not(edge))
    def _():
        pl.semaphore_wait(barrier, rows + 2)

    def send(src, dst, send_sem, recv_sem, device):
        return pltpu.make_async_remote_copy(
            src_ref=src, dst_ref=dst, send_sem=send_sem, recv_sem=recv_sem, device_id=device, device_id_type=MESH
        )

    def part(r):
        return pl.ds(pl.multiple_of(r * depth, depth), depth)

    def panel(src):
        return 2 * src + core

    def z_diag(src, way, own):
        piece = dbuf.at[panel(src), part(row)]
        return send(diag_left if own else piece, piece, s_zd.at[src, way], r_zd.at[src], column(me + 4 * way - 2))

    def z_tile(src, way):
        piece = pbuf.at[panel(src)]
        return send(piece, piece, s_zp.at[src, way], r_zp.at[src], column(me + 4 * way - 2))

    def x_diag(src, d, own):
        piece = dbuf.at[panel(src), part(row)]
        return send(diag_left if own else piece, piece, s_xd.at[src, d - 1], r_xd.at[src, d - 1], peer(d))

    def x_arrived(src, d):
        piece = dbuf.at[panel(src), part(lax.rem(row + rows - d, rows))]
        return send(piece, piece, s_xd.at[src, d - 1], r_xd.at[src, d - 1], peer(d))

    def c_tile(src, index):
        piece = pbuf.at[index]
        return send(piece, piece, s_cp.at[src], r_cp.at[src], column(partner))

    def c_diag(src, index):
        piece = dbuf.at[index]
        return send(piece, piece, s_cd.at[src], r_cd.at[src], column(partner))

    def onward(act, src, step):
        if step >= 0:

            @pl.when(chip < chips - 1)
            def _():
                act(src, 1)

        if step <= 0:

            @pl.when(chip > 0)
            def _():
                act(src, 0)

    def sources(distance):
        return ((chip, 0),) if distance == 0 else ((chip - distance, distance), (chip + distance, -distance))

    def valid(src):
        return jnp.logical_and(src >= 0, src < chips)

    def each(distance, act):
        for src, step in sources(distance):
            if distance == 0:
                act(src, step)
            else:

                @pl.when(valid(src))
                def _():
                    act(src, step)

    def spread_diag(src, step):
        own = step == 0
        if not own:
            z_diag(src, 0, False).wait_recv()
        onward(lambda s, way: z_diag(s, way, own).start(), src, step)
        for d in peers:
            x_diag(src, d, own).start()

    def spread_tile(src, step):
        if step != 0:
            z_tile(src, 0).wait_recv()
        onward(lambda s, way: z_tile(s, way).start(), src, step)
        c_tile(src, panel(src)).start()

    def complete_diag(src, step):
        for d in peers:
            x_arrived(src, d).wait_recv()
        c_diag(src, panel(src)).start()

    def add(src, step):
        accumulate(total, pbuf.at[panel(src)], dbuf.at[panel(src)], False)
        other = 2 * src + 1 - core
        c_tile(src, other).wait_recv()
        c_diag(src, other).wait_recv()
        accumulate(total, pbuf.at[other], dbuf.at[other], False)

    def finish(src, step):
        onward(lambda s, way: z_diag(s, way, step == 0).wait_send(), src, step)
        onward(lambda s, way: z_tile(s, way).wait_send(), src, step)
        for d in peers:
            x_diag(src, d, step == 0).wait_send()
        c_tile(src, panel(src)).wait_send()
        c_diag(src, panel(src)).wait_send()

    for d in peers:
        send(diag_right, full.at[part(row)], s_full.at[d - 1], r_full.at[d - 1], peer(d)).start()
    each(0, spread_diag)
    dbuf[me, part(row), :] = diag_left[...]
    full[part(row), :] = diag_right[...]
    for d in peers:
        source = full.at[part(lax.rem(row + rows - d, rows))]
        send(source, source, s_full.at[d - 1], r_full.at[d - 1], peer(d)).wait_recv()
    coupling = dot(tile_right[...], full[...], TN, HIGH) * weight[...]
    pbuf[me] = dot(tile_left[...], coupling, NN, HIGH)
    each(0, spread_tile)
    accumulate(total, old_left, old_right, True)
    each(0, complete_diag)
    for distance in range(1, chips):
        each(distance, spread_diag)
        each(distance, spread_tile)
        each(distance - 1, add)
        each(distance, complete_diag)
    each(chips - 1, add)
    split_into(total.at[0], high, low, 0)
    split_into(total.at[1], high, low, 1)
    for d in peers:
        send(diag_right, full.at[part(row)], s_full.at[d - 1], r_full.at[d - 1], peer(d)).wait_send()
    for distance in range(chips):
        each(distance, finish)


def local_kernel(high, low, start_ref, left_ref, right_ref, block):
    block[...] = start_ref[...]
    iterate(high, low, block, left_ref, right_ref)


def gathered(mesh_shape, tile_left, tile_right, diag_left, diag_right, weight, old_left, old_right):
    rows, past = mesh_shape["rows"], mesh_shape["past"]
    order, width = tile_left.shape
    vmem = pl.BlockSpec(memory_space=pltpu.VMEM)
    shape = jax.ShapeDtypeStruct((2, order, order), BF16)
    dma = pltpu.SemaphoreType.DMA
    chips = past // 2
    return pl.pallas_call(
        functools.partial(gather_kernel, rows, past),
        out_shape=(shape, shape),
        in_specs=[vmem] * 7,
        out_specs=(vmem, vmem),
        scratch_shapes=[
            pltpu.VMEM((past, order, width), F32),
            pltpu.VMEM((past, order, width), F32),
            pltpu.VMEM((order, width), F32),
            pltpu.VMEM((2, order, order), F32),
            dma((rows - 1,)), dma((rows - 1,)),
            dma((chips, 2)), dma((chips,)),
            dma((chips, 2)), dma((chips,)),
            dma((chips, rows - 1)), dma((chips, rows - 1)),
            dma((chips,)), dma((chips,)),
            dma((chips,)), dma((chips,)),
        ],
        compiler_params=pltpu.CompilerParams(
            collective_id=0, has_side_effects=True, vmem_limit_bytes=56 * 2**20
        ),
    )(tile_left, tile_right, diag_left, diag_right, weight, old_left, old_right)


def summed(tile_left, tile_right, diag_left, diag_right, weight, old_left, old_right):
    diag_left = lax.all_gather(diag_left, "rows", axis=0, tiled=True)
    diag_right = lax.all_gather(diag_right, "rows", axis=0, tiled=True)
    coupling = jnp.dot(tile_right.T, diag_right, precision=HIGH) * weight[0, 0]
    middle = jnp.dot(tile_left, coupling, precision=HIGH)
    past = lax.psum(jnp.dot(middle, diag_left.T, precision=HIGH), "past")
    total = jnp.dot(old_left, old_right.T, precision=HIGH) - past
    return halves(jnp.stack([total, total.T]))


def shards(mesh_shape, tile_left, tile_right, diag_left, diag_right, present, old_left, old_right, start):
    order, width = start.shape[1:]
    past = mesh_shape["past"]
    weight = jnp.broadcast_to(present.astype(F32), (1, width))
    terms = (tile_left[0, 0], tile_right[0, 0], diag_left[0], diag_right[0], weight, old_left[0], old_right[0])
    if past % 2 == 0 and mesh_shape["rows"] > 1 and 8 * past * order * width <= 16 * 2**20:
        high, low = gathered(mesh_shape, *terms)
    else:
        high, low = summed(*terms)
    shape = jax.ShapeDtypeStruct((order, width), F32)
    vmem = pl.BlockSpec(memory_space=pltpu.VMEM)
    left, right = pl.pallas_call(
        local_kernel,
        out_shape=(shape, shape),
        in_specs=[vmem] * 3,
        out_specs=(vmem, vmem),
        scratch_shapes=[pltpu.VMEM((order, width), F32)],
        compiler_params=pltpu.CompilerParams(vmem_limit_bytes=48 * 2**20),
    )(high, low, start[0])
    return left[None], right[None]


def solution(mesh):
    placed = (
        P("rows", "past", None, None),
        P("rows", "past", None, None),
        P("past", "rows", None),
        P("past", "rows", None),
        P("rows", "past"),
        P("rows", None, None),
        P("rows", None, None),
        P("rows", None, None),
    )
    return jax.shard_map(
        functools.partial(shards, dict(mesh.shape)),
        mesh=mesh,
        in_specs=placed,
        out_specs=(P("rows", None, None), P("rows", None, None)),
        check_vma=False,
    )
```

```python
import functools
import math

import jax
import jax.numpy as jnp
from jax import lax
from jax.experimental import pallas as pl
from jax.experimental.pallas import tpu as pltpu
from jax.sharding import PartitionSpec as P

ITERS = 3
HIGH = lax.Precision.HIGHEST
F32 = jnp.float32
BF16 = jnp.bfloat16
MESH = pl.DeviceIdType.MESH
NN = (((1,), (0,)), ((), ()))
NT = (((1,), (1,)), ((), ()))
TN = (((0,), (0,)), ((), ()))


def halves(value):
    high = value.astype(BF16)
    return high, (value - high.astype(F32)).astype(BF16)


def dot(left, right, dims, precision=None):
    return lax.dot_general(left, right, dims, precision=precision, preferred_element_type=F32)


def wide_nt(left, right):
    lh, ll = halves(left)
    rh, rl = halves(right)
    return dot(jnp.concatenate([lh, lh, ll], 1), jnp.concatenate([rh, rl, rh], 1), NT)


def gram_of(value):
    width = value.shape[1]
    high, low = halves(value)
    both = dot(high, jnp.concatenate([high, low], 1), TN)
    cross = both[:, width:]
    return both[:, :width] + (cross + cross.T)


def lower_inverse(gram):
    size = gram.shape[0]
    step = 8
    lane = lax.broadcasted_iota(jnp.int32, (step, size), 1)
    sub = lax.broadcasted_iota(jnp.int32, (step, size), 0)
    rows = [gram[step * b : step * (b + 1)] for b in range(size // step)]
    out = []

    def all_rows(value, i):
        return jnp.broadcast_to(value[i : i + 1], (step, size))

    def all_lanes(value, k):
        return jnp.broadcast_to(value[:, k : k + 1], (step, size))

    for b in range(size // step):
        base = step * b
        own = rows[b]
        inside = jnp.logical_and(lane >= base, lane < base + step)
        start = jnp.where(inside, jnp.where(lane - base == sub, 1.0, 0.0), own)
        begun = [all_rows(start, k) for k in range(step)]
        columns = [all_lanes(own, base + k) for k in range(step)]
        a = {(i, k): all_rows(columns[k], i) for k in range(step) for i in range(k, step)}
        n = {}
        for k in range(step):
            root = lax.rsqrt(a[k, k])
            for j in range(k):
                n[k, j] = n[k, j] * root
            n[k, k] = root
            scaled = {i: a[i, k] * root for i in range(k + 1, step)}
            for i in range(k + 1, step):
                for j in range(k + 1, i + 1):
                    a[i, j] = a[i, j] - scaled[i] * scaled[j]
                for j in range(k):
                    n[i, j] = n[i, j] - scaled[i] * n[k, j]
                n[i, k] = -scaled[i] * root
        done = []
        for m in range(step):
            value = n[m, 0] * begun[0]
            for j in range(1, m + 1):
                value = value + n[m, j] * begun[j]
            done.append(value)
        own = done[0]
        for m in range(1, step):
            own = jnp.where(sub == m, done[m], own)
        out.append(jnp.where(lane < base + step, own, 0.0))
        if b + 1 == size // step:
            break
        solved = []
        for k in range(step):
            value = n[k, k] * done[k]
            for m in range(k + 1, step):
                value = value + n[m, k] * done[m]
            solved.append(value)
        for t in range(b + 1, size // step):
            value = all_lanes(rows[t], base) * solved[0]
            for k in range(1, step):
                value = value + all_lanes(rows[t], base + k) * solved[k]
            rows[t] = jnp.where(inside, 0.0, rows[t]) - value
    return jnp.concatenate(out, 0)


def split_into(total_ref, high_ref, low_ref, index):
    order = total_ref.shape[0]
    tile = 128

    def body(t, carry):
        at = pl.ds(pl.multiple_of(t * tile, tile), tile)
        high, low = halves(total_ref[at, :])
        high_ref[index, at, :] = high
        low_ref[index, at, :] = low
        return carry

    lax.fori_loop(0, order // tile, body, 0)


def apply_matrix(high_ref, low_ref, index, block, out_ref):
    order, width = block.shape
    bh, bl = halves(block)
    both = jnp.concatenate([bh, bl], 1)
    tile = order // 2

    def body(t, carry):
        at = pl.ds(pl.multiple_of(t * tile, tile), tile)
        first = dot(high_ref[index, at, :], both, NN)
        second = dot(low_ref[index, at, :], bh, NN)
        out_ref[at, :] = first[:, :width] + (first[:, width:] + second)
        return carry

    lax.fori_loop(0, order // tile, body, 0)


def iterate(high_ref, low_ref, block_ref, left_ref, right_ref):
    order, width = block_ref.shape

    def step(t, carry):
        apply_matrix(high_ref, low_ref, lax.rem(t, 2), block_ref[...], right_ref)
        value = right_ref[...]
        inverse = lower_inverse(gram_of(value))
        block_ref[...] = wide_nt(value, inverse)
        return carry

    lax.fori_loop(0, 2 * ITERS + 1, step, 0)
    left_ref[...] = block_ref[...] * math.sqrt(order)
    apply_matrix(high_ref, low_ref, 1, block_ref[...], right_ref)


def accumulate(total_ref, left_ref, right_ref, first):
    order = left_ref.shape[0]
    tile = 256
    for index, (one, other) in enumerate(((left_ref, right_ref), (right_ref, left_ref))):
        oh, ol = halves(other[...])
        wide = jnp.concatenate([oh, ol, oh], 1)

        def body(t, carry):
            at = pl.ds(pl.multiple_of(t * tile, tile), tile)
            high, low = halves(one[at, :])
            value = dot(jnp.concatenate([high, high, low], 1), wide, NT)
            total_ref[index, at, :] = value if first else total_ref[index, at, :] - value
            return carry

        lax.fori_loop(0, order // tile, body, 0)


def gather_kernel(
    rows, past, tile_left, tile_right, diag_left, diag_right, weight, old_left, old_right, high, low,
    pbuf, dbuf, full, total,
    s_full, r_full, s_zd, r_zd, s_zp, r_zp, s_xd, r_xd, s_cp, r_cp, s_cd, r_cd,
):
    row = lax.axis_index("rows")
    me = lax.axis_index("past")
    core = lax.rem(me, 2)
    chip = me // 2
    chips = past // 2
    partner = me + 1 - 2 * core
    depth = diag_left.shape[0]
    peers = range(1, rows)

    def peer(d):
        return {"rows": lax.rem(row + d, rows), "past": me}

    def column(p):
        return {"rows": row, "past": p}

    barrier = pltpu.get_barrier_semaphore()
    for d in peers:
        pl.semaphore_signal(barrier, inc=1, device_id=peer(d), device_id_type=MESH)
    pl.semaphore_signal(barrier, inc=1, device_id=column(partner), device_id_type=MESH)

    @pl.when(chip > 0)
    def _():
        pl.semaphore_signal(barrier, inc=1, device_id=column(me - 2), device_id_type=MESH)

    @pl.when(chip < chips - 1)
    def _():
        pl.semaphore_signal(barrier, inc=1, device_id=column(me + 2), device_id_type=MESH)

    edge = jnp.logical_or(chip == 0, chip == chips - 1)

    @pl.when(edge)
    def _():
        pl.semaphore_wait(barrier, rows + min(chips - 1, 1))

    @pl.when(jnp.logical_not(edge))
    def _():
        pl.semaphore_wait(barrier, rows + 2)

    def send(src, dst, send_sem, recv_sem, device):
        return pltpu.make_async_remote_copy(
            src_ref=src, dst_ref=dst, send_sem=send_sem, recv_sem=recv_sem, device_id=device, device_id_type=MESH
        )

    def part(r):
        return pl.ds(pl.multiple_of(r * depth, depth), depth)

    def panel(src):
        return 2 * src + core

    def z_diag(src, way, own):
        piece = dbuf.at[panel(src), part(row)]
        return send(diag_left if own else piece, piece, s_zd.at[src, way], r_zd.at[src], column(me + 4 * way - 2))

    def z_tile(src, way):
        piece = pbuf.at[panel(src)]
        return send(piece, piece, s_zp.at[src, way], r_zp.at[src], column(me + 4 * way - 2))

    def x_diag(src, d, own):
        piece = dbuf.at[panel(src), part(row)]
        return send(diag_left if own else piece, piece, s_xd.at[src, d - 1], r_xd.at[src, d - 1], peer(d))

    def x_arrived(src, d):
        piece = dbuf.at[panel(src), part(lax.rem(row + rows - d, rows))]
        return send(piece, piece, s_xd.at[src, d - 1], r_xd.at[src, d - 1], peer(d))

    def c_tile(src, index):
        piece = pbuf.at[index]
        return send(piece, piece, s_cp.at[src], r_cp.at[src], column(partner))

    def c_diag(src, index):
        piece = dbuf.at[index]
        return send(piece, piece, s_cd.at[src], r_cd.at[src], column(partner))

    def onward(act, src, step):
        if step >= 0:

            @pl.when(chip < chips - 1)
            def _():
                act(src, 1)

        if step <= 0:

            @pl.when(chip > 0)
            def _():
                act(src, 0)

    def sources(distance):
        return ((chip, 0),) if distance == 0 else ((chip - distance, distance), (chip + distance, -distance))

    def valid(src):
        return jnp.logical_and(src >= 0, src < chips)

    def each(distance, act):
        for src, step in sources(distance):
            if distance == 0:
                act(src, step)
            else:

                @pl.when(valid(src))
                def _():
                    act(src, step)

    def spread_diag(src, step):
        own = step == 0
        if not own:
            z_diag(src, 0, False).wait_recv()
        onward(lambda s, way: z_diag(s, way, own).start(), src, step)
        for d in peers:
            x_diag(src, d, own).start()

    def spread_tile(src, step):
        if step != 0:
            z_tile(src, 0).wait_recv()
        onward(lambda s, way: z_tile(s, way).start(), src, step)
        c_tile(src, panel(src)).start()

    def complete_diag(src, step):
        for d in peers:
            x_arrived(src, d).wait_recv()
        c_diag(src, panel(src)).start()

    def add(src, step):
        accumulate(total, pbuf.at[panel(src)], dbuf.at[panel(src)], False)
        other = 2 * src + 1 - core
        c_tile(src, other).wait_recv()
        c_diag(src, other).wait_recv()
        accumulate(total, pbuf.at[other], dbuf.at[other], False)

    def finish(src, step):
        onward(lambda s, way: z_diag(s, way, step == 0).wait_send(), src, step)
        onward(lambda s, way: z_tile(s, way).wait_send(), src, step)
        for d in peers:
            x_diag(src, d, step == 0).wait_send()
        c_tile(src, panel(src)).wait_send()
        c_diag(src, panel(src)).wait_send()

    for d in peers:
        send(diag_right, full.at[part(row)], s_full.at[d - 1], r_full.at[d - 1], peer(d)).start()
    each(0, spread_diag)
    dbuf[me, part(row), :] = diag_left[...]
    full[part(row), :] = diag_right[...]
    for d in peers:
        source = full.at[part(lax.rem(row + rows - d, rows))]
        send(source, source, s_full.at[d - 1], r_full.at[d - 1], peer(d)).wait_recv()
    coupling = dot(tile_right[...], full[...], TN, HIGH) * weight[...]
    pbuf[me] = dot(tile_left[...], coupling, NN, HIGH)
    each(0, spread_tile)
    accumulate(total, old_left, old_right, True)
    each(0, complete_diag)
    for distance in range(1, chips):
        each(distance, spread_diag)
        each(distance, spread_tile)
        each(distance - 1, add)
        each(distance, complete_diag)
    each(chips - 1, add)
    split_into(total.at[0], high, low, 0)
    split_into(total.at[1], high, low, 1)
    for d in peers:
        send(diag_right, full.at[part(row)], s_full.at[d - 1], r_full.at[d - 1], peer(d)).wait_send()
    for distance in range(chips):
        each(distance, finish)


def local_kernel(high, low, start_ref, left_ref, right_ref, block):
    block[...] = start_ref[...]
    iterate(high, low, block, left_ref, right_ref)


def gathered(mesh_shape, tile_left, tile_right, diag_left, diag_right, weight, old_left, old_right):
    rows, past = mesh_shape["rows"], mesh_shape["past"]
    order, width = tile_left.shape
    vmem = pl.BlockSpec(memory_space=pltpu.VMEM)
    shape = jax.ShapeDtypeStruct((2, order, order), BF16)
    dma = pltpu.SemaphoreType.DMA
    chips = past // 2
    return pl.pallas_call(
        functools.partial(gather_kernel, rows, past),
        out_shape=(shape, shape),
        in_specs=[vmem] * 7,
        out_specs=(vmem, vmem),
        scratch_shapes=[
            pltpu.VMEM((past, order, width), F32),
            pltpu.VMEM((past, order, width), F32),
            pltpu.VMEM((order, width), F32),
            pltpu.VMEM((2, order, order), F32),
            dma((rows - 1,)), dma((rows - 1,)),
            dma((chips, 2)), dma((chips,)),
            dma((chips, 2)), dma((chips,)),
            dma((chips, rows - 1)), dma((chips, rows - 1)),
            dma((chips,)), dma((chips,)),
            dma((chips,)), dma((chips,)),
        ],
        compiler_params=pltpu.CompilerParams(
            collective_id=0, has_side_effects=True, vmem_limit_bytes=56 * 2**20
        ),
    )(tile_left, tile_right, diag_left, diag_right, weight, old_left, old_right)


def summed(tile_left, tile_right, diag_left, diag_right, weight, old_left, old_right):
    diag_left = lax.all_gather(diag_left, "rows", axis=0, tiled=True)
    diag_right = lax.all_gather(diag_right, "rows", axis=0, tiled=True)
    coupling = jnp.dot(tile_right.T, diag_right, precision=HIGH) * weight[0, 0]
    middle = jnp.dot(tile_left, coupling, precision=HIGH)
    past = lax.psum(jnp.dot(middle, diag_left.T, precision=HIGH), "past")
    total = jnp.dot(old_left, old_right.T, precision=HIGH) - past
    return halves(jnp.stack([total, total.T]))


def shards(mesh_shape, tile_left, tile_right, diag_left, diag_right, present, old_left, old_right, start):
    order, width = start.shape[1:]
    past = mesh_shape["past"]
    weight = jnp.broadcast_to(present.astype(F32), (1, width))
    terms = (tile_left[0, 0], tile_right[0, 0], diag_left[0], diag_right[0], weight, old_left[0], old_right[0])
    if past % 2 == 0 and mesh_shape["rows"] > 1 and 8 * past * order * width <= 16 * 2**20:
        high, low = gathered(mesh_shape, *terms)
    else:
        high, low = summed(*terms)
    shape = jax.ShapeDtypeStruct((order, width), F32)
    vmem = pl.BlockSpec(memory_space=pltpu.VMEM)
    left, right = pl.pallas_call(
        local_kernel,
        out_shape=(shape, shape),
        in_specs=[vmem] * 3,
        out_specs=(vmem, vmem),
        scratch_shapes=[pltpu.VMEM((order, width), F32)],
        compiler_params=pltpu.CompilerParams(vmem_limit_bytes=48 * 2**20),
    )(high, low, start[0])
    return left[None], right[None]


def solution(mesh):
    placed = (
        P("rows", "past", None, None),
        P("rows", "past", None, None),
        P("past", "rows", None),
        P("past", "rows", None),
        P("rows", "past"),
        P("rows", None, None),
        P("rows", None, None),
        P("rows", None, None),
    )
    return jax.shard_map(
        functools.partial(shards, dict(mesh.shape)),
        mesh=mesh,
        in_specs=placed,
        out_specs=(P("rows", None, None), P("rows", None, None)),
        check_vma=False,
    )
```
